32 devices in a mesh: expert: 16 (over z, x, core), tensor: 2 (over y).
Axes of the slice: x: 2, y: 2, z: 4, core: 2. Of those that a mesh axis runs over, the one named last changes fastest.
Arguments:
- attn_out: bfloat16 [2048, 4096], P('expert', 'tensor'), may hold values from -6 to 6
- residual: bfloat16 [2048, 4096], P('expert'), may hold values from -6 to 6
- o_weight: bfloat16 [4096, 4096], P('tensor'), may hold values from -0.09375 to 0.09375
- norm_gain: float32 [4096], replicated, may hold values from 0.5 to 1.5
- router_weight: bfloat16 [4096, 16], replicated, may hold values from -0.09375 to 0.09375
- expert_idx: int32 [2048, 8], P('expert'), may hold values from 0 to 15, all different within a row; in each aligned block of 64 rows (0 to 63, 64 to 127, ...) at most 48 rows name the same one
- combine: float32 [2048, 8], P('expert'), may hold values from 0.05 to 0.25
- w_gate: bfloat16 [16, 4096, 1536], P('expert', None, 'tensor'), may hold values from -0.09375 to 0.09375
- w_up: bfloat16 [16, 4096, 1536], P('expert', None, 'tensor'), may hold values from -0.09375 to 0.09375
- w_down: bfloat16 [16, 1536, 4096], P('expert', 'tensor'), may hold values from -0.15625 to 0.15625
Outputs:
- mixed: bfloat16 [2048, 4096], P('expert')
- router_logits: float32 [2048, 16], P('expert')
The draws below stay inside these ranges and needn't reach their ends.
Inputs may be any that keep to these rules, and one draw needn't show every extreme that they name: `expert_idx`: each row names 8 different experts. In each aligned block of 64 tokens no expert is named by more than 48 tokens, a bound that some block reaches.
All inputs are finite; a program needn't handle non-finite values.
Results may differ from the reference program's by a relative error of at most 0.015.
Values may be sent and summed in bfloat16 or wider, within the bound.
A program may use at most 128 MiB of HBM per device.

```python
import math
import jax
import jax.numpy as jnp
import numpy as np
from jax import lax

D = 4096
HQ = 32
HD = 128
FF = 1536
TOP = 8
TOKENS = 2048
EXPERTS = 16
ROWS = 64
CAP = 48
N_TENSOR = 2


def level_of(rng, extent, shards, low, top_value):
    loudness = 1.0
    for axis_at, blocks in shards:
        draws = jax.random.uniform(jax.random.fold_in(jax.random.fold_in(rng, 6), axis_at), (blocks,), jnp.float32, low / len(shards), top_value / len(shards))
        loudness = loudness * jnp.repeat(jnp.exp(draws), extent[axis_at] // blocks).reshape((-1,) + (1,) * (len(extent) - 1 - axis_at))
    return loudness


def deal_out(rng, own, number, rows, amount, top, most, lean):
    sequence = jax.random.permutation(rng, amount)
    crowded, common = load_shares(amount, rows * top, most, lean, True), load_shares(amount, rows * top, most, lean, False)
    places = jnp.arange(amount)

    def named(lengths, offset_by):
        used = int((lengths > 0).sum())
        fixed = max(1, used // 4)
        shifted = fixed + (places - fixed + offset_by * (used - fixed)) % max(1, amount - fixed)
        return jnp.zeros((amount,), jnp.int32).at[sequence[jnp.where(places < fixed, places, shifted)]].set(jnp.asarray(lengths, jnp.int32))

    lengths = jnp.where(number % 4 == 0, named(crowded, number // 4), named(common, number - number // 4 - 1))
    mixed = jax.random.permutation(jax.random.fold_in(own, 3), amount)
    source_of, sink = mixed[0:amount // 2 * 2:2], mixed[1:amount // 2 * 2:2]
    margin = jnp.minimum(lengths[source_of] - 1, most - lengths[sink]) // 2
    margin = jnp.where((source_of == sequence[0]) | (sink == sequence[0]) | (lengths[sink] == 0), 0, jnp.maximum(margin, 0))
    shifted = jax.random.randint(jax.random.fold_in(own, 4), (amount // 2,), 0, 1 << 20) % (margin + 1)
    lengths = lengths.at[source_of].add(-shifted).at[sink].add(shifted)
    labels = jnp.searchsorted(jnp.cumsum(lengths), jnp.arange(rows * top), side="right").astype(jnp.int32)
    table = labels.reshape(top, rows).T
    table = table[jax.random.permutation(jax.random.fold_in(own, 1), rows)]
    offset_by = jax.random.randint(jax.random.fold_in(own, 2), (rows, 1), 0, top)
    return jnp.take_along_axis(table, (jnp.arange(top)[None, :] + offset_by) % top, axis=1)


def load_shares(amount, total, limit, slope, full):
    weights = [(1 << 20) // math.isqrt(standing ** slope) + 1 for standing in range(1, amount + 1)]
    largest = limit if full else min(limit, max(-(-total // amount), total * weights[0] // sum(weights)))
    least = 1 if total - largest >= amount - 1 else 0
    holding, spare = [largest] + [least] * (amount - 1), total - largest - least * (amount - 1)
    while spare > 0:
        candidates = [i for i in range(1, amount) if holding[i] < largest] or [i for i in range(1, amount) if holding[i] < limit]
        mass, left = sum([weights[i] for i in candidates]), spare
        for i in candidates:
            more = min(limit - holding[i], max(1, left * weights[i] // mass), spare)
            holding[i] = holding[i] + more
            spare = spare - more
    return np.array(holding)


def noise(rng, dims, scale, bound, cuts=(), kind=jnp.bfloat16):
    entries = scale * jax.random.normal(rng, dims, jnp.float32)
    if cuts:
        entries = entries * level_of(rng, dims, cuts, -0.22, 0.18)
    return jnp.clip(entries, -bound, bound).astype(kind)


def setup_inputs(seed: int = 0) -> dict:
    keys = jax.random.split(jax.random.key(seed), 11)
    attn_out = noise(keys[0], (TOKENS, HQ * HD), 1.0, 6.0, ((0, 16), (1, 2)))
    residual = noise(keys[1], (TOKENS, D), 1.0, 6.0, ((0, 16),))
    o_weight = noise(keys[2], (HQ * HD, D), (HQ * HD) ** -0.5, 0.09375, ((0, 2),))
    norm_gain = jnp.clip(1.0 + 0.1 * jax.random.normal(keys[3], (D,), jnp.float32), 0.5, 1.5)
    router_weight = noise(keys[4], (D, EXPERTS), D ** -0.5, 0.09375)
    expert_idx_keys = jax.random.split(jax.random.fold_in(keys[5], 1), TOKENS // ROWS)
    expert_idx_turns = jax.random.permutation(jax.random.fold_in(keys[5], 3), TOKENS // ROWS)
    expert_idx = jax.vmap(lambda own, number: deal_out(jax.random.fold_in(keys[5], 2), own, number, ROWS, EXPERTS, TOP, CAP, 2))(expert_idx_keys, expert_idx_turns).reshape((TOKENS, TOP))
    combine = jnp.clip(0.05 + 0.2 * jax.random.uniform(keys[6], (TOKENS, TOP), jnp.float32) ** level_of(keys[6], (TOKENS, TOP), ((0, 16),), -0.2, 0.2), 0.05, 0.25)
    w_gate = noise(keys[7], (EXPERTS, D, FF), D ** -0.5, 0.09375, ((0, 16), (2, 2)))
    w_up = noise(keys[8], (EXPERTS, D, FF), D ** -0.5, 0.09375, ((0, 16), (2, 2)))
    w_down = noise(keys[9], (EXPERTS, FF, D), FF ** -0.5, 0.15625, ((0, 16), (1, 2)))
    return {"attn_out": attn_out, "residual": residual, "o_weight": o_weight, "norm_gain": norm_gain, "router_weight": router_weight, "expert_idx": expert_idx, "combine": combine, "w_gate": w_gate, "w_up": w_up, "w_down": w_down}


epsilon = 1e-06

def reference(attn_out, residual, o_weight, norm_gain, router_weight, expert_idx, combine, w_gate, w_up, w_down):
    projected = jnp.dot(attn_out, o_weight, preferred_element_type=jnp.float32)
    stream = (residual.astype(jnp.float32) + projected).astype(jnp.bfloat16)
    stream_wide = stream.astype(jnp.float32)
    scale = lax.rsqrt(lax.optimization_barrier(jnp.mean(stream_wide * stream_wide, axis=-1, keepdims=True)) + epsilon)
    normed = (stream_wide * scale * norm_gain.astype(jnp.float32)).astype(jnp.bfloat16)
    router_logits = jnp.dot(normed, router_weight, preferred_element_type=jnp.float32)
    block_count = TOKENS // ROWS
    flat_ids = expert_idx.reshape(block_count, ROWS * TOP)
    one_hot = (flat_ids[:, :, None] == jnp.arange(EXPERTS, dtype=jnp.int32)[None, None, :]).astype(jnp.int32)
    slot_index = lax.optimization_barrier(jnp.sum((jnp.cumsum(one_hot, axis=1) - 1) * one_hot, axis=2)).astype(jnp.int32)
    block_ids = jnp.broadcast_to(jnp.arange(block_count, dtype=jnp.int32)[:, None], (block_count, ROWS * TOP))
    token_rows = jnp.repeat(jnp.arange(TOKENS, dtype=jnp.int32), TOP)
    expert_in = jnp.zeros((EXPERTS, block_count, CAP, D), jnp.bfloat16)
    expert_in = expert_in.at[flat_ids.reshape(-1), block_ids.reshape(-1), slot_index.reshape(-1)].set(normed[token_rows])

    def one_expert(operands):
        rows_in, gate_w, up_w, down_w = operands
        flat_rows = rows_in.reshape(block_count * CAP, D)
        gate = jnp.dot(flat_rows, gate_w, preferred_element_type=jnp.float32)
        up_val = jnp.dot(flat_rows, up_w, preferred_element_type=jnp.float32)
        hidden = (jax.nn.silu(gate) * up_val).astype(jnp.bfloat16)
        grouped = hidden.reshape(block_count * CAP, N_TENSOR, FF // N_TENSOR).astype(jnp.float32)
        down_grouped = down_w.reshape(N_TENSOR, FF // N_TENSOR, D).astype(jnp.float32)
        partials = jnp.einsum('sgf,gfd->gsd', grouped, down_grouped).astype(jnp.bfloat16)
        total = lax.optimization_barrier(jnp.sum(partials.astype(jnp.float32), axis=0)).astype(jnp.bfloat16)
        return total.reshape(block_count, CAP, D)
    expert_out = lax.map(one_expert, (expert_in, w_gate, w_up, w_down))
    token_block = (jnp.arange(TOKENS, dtype=jnp.int32) // ROWS)[:, None]
    picked = expert_out[expert_idx, jnp.broadcast_to(token_block, (TOKENS, TOP)), slot_index.reshape(TOKENS, TOP)]
    moe = lax.optimization_barrier(jnp.sum(combine[:, :, None] * picked.astype(jnp.float32), axis=1))
    mixed = (stream.astype(jnp.float32) + moe).astype(jnp.bfloat16)
    return (mixed, router_logits)
```

```python
import jax
import jax.numpy as jnp
from jax import lax
from jax.sharding import PartitionSpec as P

epsilon = 1e-06


def rms_scaled(stream, norm_gain):
    wide = stream.astype(jnp.float32)
    scale = lax.rsqrt(jnp.mean(wide * wide, axis=-1, keepdims=True) + epsilon)
    return (wide * scale * norm_gain).astype(jnp.bfloat16)


def shards(
    attn_out,
    residual,
    o_weight,
    norm_gain,
    router_weight,
    expert_idx,
    combine,
    w_gate,
    w_up,
    w_down,
):
    tensor_size = lax.axis_size("tensor")
    tensor_rank = lax.axis_index("tensor")
    me = lax.axis_index("expert")
    rows_dev = residual.shape[0] // tensor_size
    expert_count = router_weight.shape[1]
    experts = jnp.arange(expert_count, dtype=jnp.int32)
    dense = jnp.sum(
        jnp.where(expert_idx[:, :, None] == experts, combine[:, :, None], 0.0), axis=1
    )
    dense_all = lax.all_gather(dense, "expert", axis=0, tiled=True)
    mine = jnp.sum(jnp.where(experts == me, dense_all, 0.0), axis=1, keepdims=True)

    projected = lax.psum_scatter(
        jnp.dot(attn_out, o_weight, preferred_element_type=jnp.float32).astype(jnp.bfloat16),
        "tensor",
        scatter_dimension=0,
        tiled=True,
    ).astype(jnp.float32)
    residual_mine = lax.dynamic_slice_in_dim(residual, tensor_rank * rows_dev, rows_dev, 0)
    stream = (residual_mine.astype(jnp.float32) + projected).astype(jnp.bfloat16)
    normed = rms_scaled(stream, norm_gain)
    every = lax.all_gather(normed, ("expert", "tensor"), axis=0, tiled=True)
    logits = jnp.dot(normed, router_weight, preferred_element_type=jnp.float32)
    gate = jnp.dot(every, w_gate[0], preferred_element_type=jnp.float32)
    up = jnp.dot(every, w_up[0], preferred_element_type=jnp.float32)
    hidden = (jax.nn.silu(gate) * up * mine).astype(jnp.bfloat16)
    part = jnp.dot(hidden, w_down[0], preferred_element_type=jnp.float32).astype(jnp.bfloat16)
    moe = lax.psum_scatter(part, ("expert", "tensor"), scatter_dimension=0, tiled=True)
    mixed = (stream.astype(jnp.float32) + moe.astype(jnp.float32)).astype(jnp.bfloat16)
    return (
        lax.all_gather(mixed, "tensor", axis=0, tiled=True),
        lax.all_gather(logits, "tensor", axis=0, tiled=True),
    )


def solution(mesh):
    in_specs = (
        P("expert", "tensor"),
        P("expert", None),
        P("tensor", None),
        P(),
        P(),
        P("expert", None),
        P("expert", None),
        P("expert", None, "tensor"),
        P("expert", None, "tensor"),
        P("expert", "tensor", None),
    )
    out_specs = (P("expert", None), P("expert", None))
    return jax.shard_map(shards, mesh=mesh, in_specs=in_specs, out_specs=out_specs, check_vma=False)
```

```python
import functools

import jax
import jax.numpy as jnp
from jax import lax
from jax.experimental import pallas as pl
from jax.experimental.pallas import tpu as pltpu
from jax.sharding import PartitionSpec as P

epsilon = 1e-06
CUTS = 8


class Place:
    def __init__(self, outer):
        e = lax.axis_index("expert")
        self.outer = outer
        self.y = lax.axis_index("tensor")
        self.c = lax.rem(e, 2)
        self.x = lax.rem(e // 2, 2)
        self.z = e // 4

    def device(self, z=None, x=None, c=None, y=None):
        z = self.z if z is None else z
        x = self.x if x is None else x
        c = self.c if c is None else c
        y = self.y if y is None else y
        return {"expert": (z * 2 + x) * 2 + c, "tensor": y}

    def far(self, j):
        return lax.rem(self.z + j, self.outer)

    def greet(self):
        barrier = pltpu.get_barrier_semaphore()
        peers = [self.device(c=1 - self.c), self.device(x=1 - self.x), self.device(y=1 - self.y)]
        peers += [self.device(z=self.far(j)) for j in range(1, self.outer)]
        for peer in peers:
            pl.semaphore_signal(barrier, inc=1, device_id=peer, device_id_type=pl.DeviceIdType.MESH)
        pl.semaphore_wait(barrier, len(peers))


def remote(src, dst, send, recv, device):
    return pltpu.make_async_remote_copy(
        src_ref=src, dst_ref=dst, send_sem=send, recv_sem=recv,
        device_id=device, device_id_type=pl.DeviceIdType.MESH,
    )


def wavefront(count, stages, lags):
    for t in range(count + lags[-1]):
        for stage, lag in zip(stages, lags):
            if 0 <= t - lag < count:
                stage(t - lag)


def scatter_kernel(outer, h_ref, w_ref, s_ref, o_ref, acc, snd, rc, r1, r2, rz, send, recv):
    at = Place(outer)
    x, y, z, c = at.x, at.y, at.z, at.c
    _, _, _, _, rows, width = acc.shape
    block = 4 * rows
    at.greet()
    copies = {}

    def go(k, s, src, dst, device):
        copies[k, s] = remote(src, dst, send.at[k, s], recv.at[k, s], device)
        copies[k, s].start()

    def each(body):
        lax.fori_loop(0, outer, lambda i, _: (body(i), 0)[1], 0)

    def products(k, part, into):
        def one(i):
            start = pl.multiple_of(part * (outer * block) + i * block, block)
            out = jnp.dot(
                h_ref[pl.ds(start, block), :],
                w_ref[:, k * width:(k + 1) * width],
                preferred_element_type=jnp.float32,
            )
            into[k, i] = out.astype(jnp.bfloat16).reshape(2, 2, rows, width)
        each(one)

    def s0(k):
        products(k, 1 - c, snd)
        go(k, 0, snd.at[k], rc.at[k], at.device(c=1 - c))
        products(k, c, acc)

    def s1(k):
        copies[k, 0].wait_recv()
        if k % 2 == 0:
            def part(v):
                def one(i):
                    acc[k, i, v] = acc[k, i, v] + rc[k, i, v]
                each(one)
            part(1 - x)
            go(k, 1, acc.at[k, :, 1 - x], r1.at[k], at.device(x=1 - x))
            part(x)
        else:
            def part(v):
                def one(i):
                    acc[k, i, :, v] = acc[k, i, :, v] + rc[k, i, :, v]
                each(one)
            part(1 - y)
            go(k, 1, acc.at[k, :, :, 1 - y], r1.at[k], at.device(y=1 - y))
            part(y)

    def s2(k):
        copies[k, 1].wait_recv()
        if k % 2 == 0:
            def part(v):
                def one(i):
                    acc[k, i, x, v] = acc[k, i, x, v] + r1[k, i, v]
                each(one)
            part(1 - y)
            go(k, 2, acc.at[k, :, x, 1 - y], r2.at[k], at.device(y=1 - y))
            part(y)
        else:
            def part(v):
                def one(i):
                    acc[k, i, v, y] = acc[k, i, v, y] + r1[k, i, v]
                each(one)
            part(1 - x)
            go(k, 2, acc.at[k, :, 1 - x, y], r2.at[k], at.device(x=1 - x))
            part(x)

    def s3(k):
        copies[k, 2].wait_recv()

        def one(i):
            acc[k, i, x, y] = acc[k, i, x, y] + r2[k, i]
        each(one)
        for j in range(1, outer):
            d = at.far(j)
            go(k, 3 + j, acc.at[k, d, x, y], rz.at[k, j - 1], at.device(z=d))

    def s4(k):
        cols = slice(k * width, (k + 1) * width)
        for j in range(1, outer):
            copies[k, 3 + j].wait_recv()
        total = acc[k, z, x, y].astype(jnp.float32)
        for j in range(1, outer):
            total = total + rz[k, j - 1].astype(jnp.float32)
        o_ref[y, :, cols] = (s_ref[:, cols].astype(jnp.float32) + total).astype(jnp.bfloat16)
        go(k, 3, o_ref.at[y, :, cols], o_ref.at[y, :, cols], at.device(y=1 - y))

    wavefront(CUTS, [s0, s1, s2, s3, s4], [0, 1, 3, 5, 7])
    for k in range(CUTS):
        copies[k, 3].wait_recv()
    for copy in copies.values():
        copy.wait_send()


def experts_home(hidden, w_down, stream, outer):
    rows, width = stream.shape
    cut = width // CUTS
    vmem = pl.BlockSpec(memory_space=pltpu.VMEM)
    bf16 = jnp.bfloat16
    return pl.pallas_call(
        functools.partial(scatter_kernel, outer),
        out_shape=jax.ShapeDtypeStruct((2, rows, width), bf16),
        in_specs=[vmem] * 3,
        out_specs=vmem,
        scratch_shapes=[
            pltpu.VMEM((CUTS, outer, 2, 2, rows, cut), bf16),
            pltpu.VMEM((CUTS, outer, 2, 2, rows, cut), bf16),
            pltpu.VMEM((CUTS, outer, 2, 2, rows, cut), bf16),
            pltpu.VMEM((CUTS, outer, 2, rows, cut), bf16),
            pltpu.VMEM((CUTS, outer, rows, cut), bf16),
            pltpu.VMEM((CUTS, outer - 1, rows, cut), bf16),
            pltpu.SemaphoreType.DMA((CUTS, outer + 3)),
            pltpu.SemaphoreType.DMA((CUTS, outer + 3)),
        ],
        compiler_params=pltpu.CompilerParams(
            collective_id=1, has_side_effects=True, vmem_limit_bytes=56 << 20
        ),
    )(hidden, w_down, stream)


def gather_kernel(outer, n_ref, e_ref, o_ref, eo_ref, send, recv, local):
    at = Place(outer)
    x, y, z, c = at.x, at.y, at.z, at.c
    width = n_ref.shape[1] // CUTS
    own = [
        pltpu.make_async_copy(n_ref, o_ref.at[c, z, x, y], local.at[0]),
        pltpu.make_async_copy(e_ref, eo_ref.at[c, z, x, y], local.at[1]),
    ]
    for copy in own:
        copy.start()
    at.greet()
    copies = {}

    def go(k, s, src, dst, device):
        copies[k, s] = remote(src, dst, send.at[k, s], recv.at[k, s], device)
        copies[k, s].start()

    def refs(k):
        if k == 0:
            return e_ref, eo_ref, slice(None)
        return n_ref, o_ref, pl.ds((k - 1) * width, width)

    for k in range(CUTS + 1):
        src, dst, cols = refs(k)
        for j in range(1, outer):
            go(k, 2 + j, src.at[:, cols], dst.at[c, z, x, y, :, cols], at.device(z=at.far(j)))
    for copy in own:
        copy.wait()

    def s1(k):
        for j in range(1, outer):
            copies[k, 2 + j].wait_recv()
        _, ref, cols = refs(k)
        part = ref.at[c, :, x, y, :, cols]
        go(k, 0, part, part, at.device(x=1 - x) if k % 2 else at.device(y=1 - y))

    def s2(k):
        copies[k, 0].wait_recv()
        _, ref, cols = refs(k)
        if k % 2:
            part = ref.at[c, :, :, y, :, cols]
            go(k, 1, part, part, at.device(y=1 - y))
        else:
            part = ref.at[c, :, x, :, :, cols]
            go(k, 1, part, part, at.device(x=1 - x))

    def s3(k):
        copies[k, 1].wait_recv()
        _, ref, cols = refs(k)
        part = ref.at[c, :, :, :, :, cols]
        go(k, 2, part, part, at.device(c=1 - c))

    wavefront(CUTS + 1, [s1, s2, s3], [0, 2, 4])
    for k in range(CUTS + 1):
        copies[k, 2].wait_recv()
    for copy in copies.values():
        copy.wait_send()


def gather_rows(normed, extra, outer):
    anywhere = pl.BlockSpec(memory_space=pl.ANY)
    return pl.pallas_call(
        functools.partial(gather_kernel, outer),
        out_shape=[
            jax.ShapeDtypeStruct((2, outer, 2, 2, *v.shape), v.dtype) for v in (normed, extra)
        ],
        in_specs=[anywhere] * 2,
        out_specs=[anywhere] * 2,
        scratch_shapes=[
            pltpu.SemaphoreType.DMA((CUTS + 1, outer + 2)),
            pltpu.SemaphoreType.DMA((CUTS + 1, outer + 2)),
            pltpu.SemaphoreType.DMA((2,)),
        ],
        compiler_params=pltpu.CompilerParams(collective_id=2, has_side_effects=True),
    )(normed, extra)


def rms_scaled(stream, norm_gain):
    wide = stream.astype(jnp.float32)
    scale = lax.rsqrt(jnp.mean(wide * wide, axis=-1, keepdims=True) + epsilon)
    return (wide * scale * norm_gain).astype(jnp.bfloat16)


def shards(
    attn_out,
    residual,
    o_weight,
    norm_gain,
    router_weight,
    expert_idx,
    combine,
    w_gate,
    w_up,
    w_down,
):
    tensor_size = lax.axis_size("tensor")
    tensor_rank = lax.axis_index("tensor")
    me = lax.axis_index("expert")
    rows_dev = residual.shape[0] // tensor_size
    expert_count = router_weight.shape[1]
    experts = jnp.arange(expert_count, dtype=jnp.int32)
    dense = jnp.sum(
        jnp.where(expert_idx[:, :, None] == experts, combine[:, :, None], 0.0), axis=1
    )
    dense_all = lax.all_gather(dense, "expert", axis=0, tiled=True)
    mine = jnp.sum(jnp.where(experts == me, dense_all, 0.0), axis=1, keepdims=True)

    projected = lax.psum_scatter(
        jnp.dot(attn_out, o_weight, preferred_element_type=jnp.float32).astype(jnp.bfloat16),
        "tensor",
        scatter_dimension=0,
        tiled=True,
    ).astype(jnp.float32)
    residual_mine = lax.dynamic_slice_in_dim(residual, tensor_rank * rows_dev, rows_dev, 0)
    stream = (residual_mine.astype(jnp.float32) + projected).astype(jnp.bfloat16)
    normed = rms_scaled(stream, norm_gain)
    every = lax.all_gather(normed, ("expert", "tensor"), axis=0, tiled=True)
    logits = jnp.dot(normed, router_weight, preferred_element_type=jnp.float32)
    gate = jnp.dot(every, w_gate[0], preferred_element_type=jnp.float32)
    up = jnp.dot(every, w_up[0], preferred_element_type=jnp.float32)
    hidden = (jax.nn.silu(gate) * up * mine).astype(jnp.bfloat16)
    part = jnp.dot(hidden, w_down[0], preferred_element_type=jnp.float32).astype(jnp.bfloat16)
    moe = lax.psum_scatter(part, ("expert", "tensor"), scatter_dimension=0, tiled=True)
    mixed = (stream.astype(jnp.float32) + moe.astype(jnp.float32)).astype(jnp.bfloat16)
    return (
        lax.all_gather(mixed, "tensor", axis=0, tiled=True),
        lax.all_gather(logits, "tensor", axis=0, tiled=True),
    )

def shards_paired(
    attn_out,
    residual,
    o_weight,
    norm_gain,
    router_weight,
    expert_idx,
    combine,
    w_gate,
    w_up,
    w_down,
):
    y = lax.axis_index("tensor")
    me = lax.axis_index("expert")
    outer = lax.axis_size("expert") // 4
    rows = residual.shape[0] // 2
    width = residual.shape[1]
    expert_count = router_weight.shape[1]
    bf16 = jnp.bfloat16

    def take(array, at):
        return lax.dynamic_slice_in_dim(array, at * rows, rows, 0)

    experts = jnp.arange(expert_count, dtype=jnp.int32)
    dense = jnp.sum(
        jnp.where(take(expert_idx, y)[:, :, None] == experts, take(combine, y)[:, :, None], 0.0),
        axis=1,
    )
    high = dense.astype(bf16)
    low = (dense - high.astype(jnp.float32)).astype(bf16)
    extra = jnp.pad(jnp.concatenate([high, low], axis=1), ((0, 0), (0, -2 * expert_count % 128)))

    partial = jnp.dot(attn_out, o_weight, preferred_element_type=jnp.float32).astype(bf16)
    came = lax.ppermute(take(partial, 1 - y), "tensor", [(0, 1), (1, 0)])
    projected = take(partial, y).astype(jnp.float32) + came.astype(jnp.float32)
    stream = (take(residual, y).astype(jnp.float32) + projected).astype(bf16)
    normed = rms_scaled(stream, norm_gain)
    every, extras = gather_rows(normed, extra, outer)
    group = every[me % 2, me // 4, (me // 2) % 2].reshape(2 * rows, width)
    logits = jnp.dot(group, router_weight, preferred_element_type=jnp.float32)
    every = every.reshape(-1, width)
    extras = extras.reshape(-1, extra.shape[1]).astype(jnp.float32)
    named = extras[:, :expert_count] + extras[:, expert_count:2 * expert_count]
    mine = jnp.sum(jnp.where(experts == me, named, 0.0), axis=1, keepdims=True)
    gate = jnp.dot(every, w_gate[0], preferred_element_type=jnp.float32)
    up = jnp.dot(every, w_up[0], preferred_element_type=jnp.float32)
    hidden = (jax.nn.silu(gate) * up * mine).astype(bf16)
    mixed = experts_home(hidden, w_down[0], stream, outer)
    return mixed.reshape(2 * rows, width), logits


def solution(mesh):
    in_specs = (
        P("expert", "tensor"),
        P("expert", None),
        P("tensor", None),
        P(),
        P(),
        P("expert", None),
        P("expert", None),
        P("expert", None, "tensor"),
        P("expert", None, "tensor"),
        P("expert", "tensor", None),
    )
    out_specs = (P("expert", None), P("expert", None))
    paired = mesh.shape["tensor"] == 2 and mesh.shape["expert"] % 4 == 0
    paired = paired and mesh.shape["expert"] > 4
    body = shards_paired if paired else shards
    return jax.shard_map(body, mesh=mesh, in_specs=in_specs, out_specs=out_specs, check_vma=False)
```

```python
import functools

import jax
import jax.numpy as jnp
from jax import lax
from jax.experimental import pallas as pl
from jax.experimental.pallas import tpu as pltpu
from jax.sharding import PartitionSpec as P

epsilon = 1e-06
CUTS = 8


class Place:
    def __init__(self, outer):
        e = lax.axis_index("expert")
        self.outer = outer
        self.y = lax.axis_index("tensor")
        self.c = lax.rem(e, 2)
        self.x = lax.rem(e // 2, 2)
        self.z = e // 4

    def device(self, z=None, x=None, c=None, y=None):
        z = self.z if z is None else z
        x = self.x if x is None else x
        c = self.c if c is None else c
        y = self.y if y is None else y
        return {"expert": (z * 2 + x) * 2 + c, "tensor": y}

    def far(self, j):
        return lax.rem(self.z + j, self.outer)

    def greet(self):
        barrier = pltpu.get_barrier_semaphore()
        peers = [self.device(c=1 - self.c), self.device(x=1 - self.x), self.device(y=1 - self.y)]
        peers += [self.device(z=self.far(j)) for j in range(1, self.outer)]
        for peer in peers:
            pl.semaphore_signal(barrier, inc=1, device_id=peer, device_id_type=pl.DeviceIdType.MESH)
        pl.semaphore_wait(barrier, len(peers))


def remote(src, dst, send, recv, device):
    return pltpu.make_async_remote_copy(
        src_ref=src, dst_ref=dst, send_sem=send, recv_sem=recv,
        device_id=device, device_id_type=pl.DeviceIdType.MESH,
    )


def wavefront(count, stages, lags):
    for t in range(count + lags[-1]):
        for stage, lag in zip(stages, lags):
            if 0 <= t - lag < count:
                stage(t - lag)


def scatter_kernel(outer, h_ref, w_ref, s_ref, o_ref, acc, snd, rc, r1, r2, rz, send, recv):
    at = Place(outer)
    x, y, z, c = at.x, at.y, at.z, at.c
    _, _, _, _, rows, width = acc.shape
    block = 4 * rows
    at.greet()
    copies = {}

    def go(k, s, src, dst, device):
        copies[k, s] = remote(src, dst, send.at[k, s], recv.at[k, s], device)
        copies[k, s].start()

    def each(body):
        lax.fori_loop(0, outer, lambda i, _: (body(i), 0)[1], 0)

    def products(k, part, into):
        def one(i):
            start = pl.multiple_of(part * (outer * block) + i * block, block)
            out = jnp.dot(
                h_ref[pl.ds(start, block), :],
                w_ref[:, k * width:(k + 1) * width],
                preferred_element_type=jnp.float32,
            )
            into[k, i] = out.astype(jnp.bfloat16).reshape(2, 2, rows, width)
        each(one)

    def s0(k):
        products(k, 1 - c, snd)
        go(k, 0, snd.at[k], rc.at[k], at.device(c=1 - c))
        products(k, c, acc)

    def s1(k):
        copies[k, 0].wait_recv()
        if k % 2 == 0:
            def part(v):
                def one(i):
                    acc[k, i, v] = acc[k, i, v] + rc[k, i, v]
                each(one)
            part(1 - x)
            go(k, 1, acc.at[k, :, 1 - x], r1.at[k], at.device(x=1 - x))
            part(x)
        else:
            def part(v):
                def one(i):
                    acc[k, i, :, v] = acc[k, i, :, v] + rc[k, i, :, v]
                each(one)
            part(1 - y)
            go(k, 1, acc.at[k, :, :, 1 - y], r1.at[k], at.device(y=1 - y))
            part(y)

    def s2(k):
        copies[k, 1].wait_recv()
        if k % 2 == 0:
            def part(v):
                def one(i):
                    acc[k, i, x, v] = acc[k, i, x, v] + r1[k, i, v]
                each(one)
            part(1 - y)
            go(k, 2, acc.at[k, :, x, 1 - y], r2.at[k], at.device(y=1 - y))
            part(y)
        else:
            def part(v):
                def one(i):
                    acc[k, i, v, y] = acc[k, i, v, y] + r1[k, i, v]
                each(one)
            part(1 - x)
            go(k, 2, acc.at[k, :, 1 - x, y], r2.at[k], at.device(x=1 - x))
            part(x)

    def s3(k):
        copies[k, 2].wait_recv()

        def one(i):
            acc[k, i, x, y] = acc[k, i, x, y] + r2[k, i]
        each(one)
        for j in range(1, outer):
            d = at.far(j)
            go(k, 3 + j, acc.at[k, d, x, y], rz.at[k, j - 1], at.device(z=d))

    def s4(k):
        cols = slice(k * width, (k + 1) * width)
        for j in range(1, outer):
            copies[k, 3 + j].wait_recv()
        total = acc[k, z, x, y].astype(jnp.float32)
        for j in range(1, outer):
            total = total + rz[k, j - 1].astype(jnp.float32)
        o_ref[y, :, cols] = (s_ref[:, cols].astype(jnp.float32) + total).astype(jnp.bfloat16)
        go(k, 3, o_ref.at[y, :, cols], o_ref.at[y, :, cols], at.device(y=1 - y))

    wavefront(CUTS, [s0, s1, s2, s3, s4], [0, 1, 3, 5, 7])
    for k in range(CUTS):
        copies[k, 3].wait_recv()
    for copy in copies.values():
        copy.wait_send()


def experts_home(hidden, w_down, stream, outer):
    rows, width = stream.shape
    cut = width // CUTS
    vmem = pl.BlockSpec(memory_space=pltpu.VMEM)
    bf16 = jnp.bfloat16
    return pl.pallas_call(
        functools.partial(scatter_kernel, outer),
        out_shape=jax.ShapeDtypeStruct((2, rows, width), bf16),
        in_specs=[vmem] * 3,
        out_specs=vmem,
        scratch_shapes=[
            pltpu.VMEM((CUTS, outer, 2, 2, rows, cut), bf16),
            pltpu.VMEM((CUTS, outer, 2, 2, rows, cut), bf16),
            pltpu.VMEM((CUTS, outer, 2, 2, rows, cut), bf16),
            pltpu.VMEM((CUTS, outer, 2, rows, cut), bf16),
            pltpu.VMEM((CUTS, outer, rows, cut), bf16),
            pltpu.VMEM((CUTS, outer - 1, rows, cut), bf16),
            pltpu.SemaphoreType.DMA((CUTS, outer + 3)),
            pltpu.SemaphoreType.DMA((CUTS, outer + 3)),
        ],
        compiler_params=pltpu.CompilerParams(
            collective_id=1, has_side_effects=True, vmem_limit_bytes=56 << 20
        ),
    )(hidden, w_down, stream)


def gather_kernel(
    outer, n_ref, e_ref, g_hbm, u_hbm, r_ref, h_ref, l_ref,
    every, extras, g_ref, u_ref, gate, up, send, recv, local,
):
    at = Place(outer)
    x, y, z, c = at.x, at.y, at.z, at.c
    me = lax.axis_index("expert")
    rows = n_ref.shape[0]
    width = n_ref.shape[1] // CUTS
    count = r_ref.shape[1]
    block = 4 * rows
    weights = [
        pltpu.make_async_copy(g_hbm, g_ref, local.at[0]),
        pltpu.make_async_copy(u_hbm, u_ref, local.at[1]),
    ]
    for copy in weights:
        copy.start()
    extras[c, z, x, y] = e_ref[...]
    for k in range(CUTS):
        every[k, c, z, x, y] = n_ref[:, k * width:(k + 1) * width]
    l_ref[...] = jnp.zeros_like(l_ref)
    at.greet()
    copies = {}

    def go(k, s, part, device):
        copies[k, s] = remote(part, part, send.at[k, s], recv.at[k, s], device)
        copies[k, s].start()

    def held(k):
        return extras if k == 0 else every.at[k - 1]

    def compute(k, half):
        cols = slice((k - 1) * width, k * width)

        def one(i, _):
            lhs = every[k - 1, half, i].reshape(block, width)
            g = jnp.dot(lhs, g_ref[cols, :], preferred_element_type=jnp.float32)
            u = jnp.dot(lhs, u_ref[cols, :], preferred_element_type=jnp.float32)
            if k > 1:
                g = g + gate[half, i]
                u = u + up[half, i]
            if k < CUTS:
                gate[half, i] = g
                up[half, i] = u
            else:
                pair = extras[half, i].reshape(block, -1).astype(jnp.float32)
                lane = lax.broadcasted_iota(jnp.int32, pair.shape, 1)
                chosen = (lane == me) | (lane == me + count)
                mine = jnp.sum(jnp.where(chosen, pair, 0.0), axis=1, keepdims=True)
                value = g / (1.0 + jnp.exp(-g)) * u * mine
                start = pl.multiple_of((half * outer + i) * block, block)
                h_ref[pl.ds(start, block), :] = value.astype(jnp.bfloat16)
            return 0

        lax.fori_loop(0, outer, one, 0)

    def s0(k):
        for j in range(1, outer):
            go(k, 2 + j, held(k).at[c, z, x, y], at.device(z=at.far(j)))

    def s1(k):
        for j in range(1, outer):
            copies[k, 2 + j].wait_recv()
        go(k, 0, held(k).at[c, :, x, y], at.device(x=1 - x) if k % 2 else at.device(y=1 - y))

    def s2(k):
        copies[k, 0].wait_recv()
        if k % 2:
            go(k, 1, held(k).at[c, :, :, y], at.device(y=1 - y))
        else:
            go(k, 1, held(k).at[c, :, x], at.device(x=1 - x))

    def s3(k):
        copies[k, 1].wait_recv()
        go(k, 2, held(k).at[c], at.device(c=1 - c))
        if k == 1:
            for copy in weights:
                copy.wait()
        if 0 < k < CUTS:
            compute(k, c)

    def s4(k):
        if k == CUTS:
            compute(k, c)
        if k > 0:
            group = every[k - 1, c, z, x].reshape(2 * rows, width)
            router = r_ref[(k - 1) * width:k * width, :]
            l_ref[...] += jnp.dot(group, router, preferred_element_type=jnp.float32)
        copies[k, 2].wait_recv()
        if k > 0:
            compute(k, 1 - c)

    wavefront(CUTS + 1, [s0, s1, s2, s3, s4], [0, 2, 4, 6, 7])
    for copy in copies.values():
        copy.wait_send()


def gather_hidden(normed, extra, w_gate, w_up, router, outer):
    rows, width = normed.shape
    cut = width // CUTS
    units = w_gate.shape[1]
    bf16, f32 = jnp.bfloat16, jnp.float32
    vmem = pl.BlockSpec(memory_space=pltpu.VMEM)
    anywhere = pl.BlockSpec(memory_space=pl.ANY)
    return pl.pallas_call(
        functools.partial(gather_kernel, outer),
        out_shape=[
            jax.ShapeDtypeStruct((8 * outer * rows, units), bf16),
            jax.ShapeDtypeStruct((2 * rows, router.shape[1]), f32),
        ],
        in_specs=[vmem, vmem, anywhere, anywhere, vmem],
        out_specs=[vmem] * 2,
        scratch_shapes=[
            pltpu.VMEM((CUTS, 2, outer, 2, 2, rows, cut), bf16),
            pltpu.VMEM((2, outer, 2, 2, *extra.shape), bf16),
            pltpu.VMEM((width, units), bf16),
            pltpu.VMEM((width, units), bf16),
            pltpu.VMEM((2, outer, 4 * rows, units), f32),
            pltpu.VMEM((2, outer, 4 * rows, units), f32),
            pltpu.SemaphoreType.DMA((CUTS + 1, outer + 2)),
            pltpu.SemaphoreType.DMA((CUTS + 1, outer + 2)),
            pltpu.SemaphoreType.DMA((2,)),
        ],
        compiler_params=pltpu.CompilerParams(
            collective_id=2, has_side_effects=True, vmem_limit_bytes=58 << 20
        ),
    )(normed, extra, w_gate, w_up, router)


def rms_scaled(stream, norm_gain):
    wide = stream.astype(jnp.float32)
    scale = lax.rsqrt(jnp.mean(wide * wide, axis=-1, keepdims=True) + epsilon)
    return (wide * scale * norm_gain).astype(jnp.bfloat16)


def shards(
    attn_out,
    residual,
    o_weight,
    norm_gain,
    router_weight,
    expert_idx,
    combine,
    w_gate,
    w_up,
    w_down,
):
    tensor_size = lax.axis_size("tensor")
    tensor_rank = lax.axis_index("tensor")
    me = lax.axis_index("expert")
    rows_dev = residual.shape[0] // tensor_size
    expert_count = router_weight.shape[1]
    experts = jnp.arange(expert_count, dtype=jnp.int32)
    dense = jnp.sum(
        jnp.where(expert_idx[:, :, None] == experts, combine[:, :, None], 0.0), axis=1
    )
    dense_all = lax.all_gather(dense, "expert", axis=0, tiled=True)
    mine = jnp.sum(jnp.where(experts == me, dense_all, 0.0), axis=1, keepdims=True)

    projected = lax.psum_scatter(
        jnp.dot(attn_out, o_weight, preferred_element_type=jnp.float32).astype(jnp.bfloat16),
        "tensor",
        scatter_dimension=0,
        tiled=True,
    ).astype(jnp.float32)
    residual_mine = lax.dynamic_slice_in_dim(residual, tensor_rank * rows_dev, rows_dev, 0)
    stream = (residual_mine.astype(jnp.float32) + projected).astype(jnp.bfloat16)
    normed = rms_scaled(stream, norm_gain)
    every = lax.all_gather(normed, ("expert", "tensor"), axis=0, tiled=True)
    logits = jnp.dot(normed, router_weight, preferred_element_type=jnp.float32)
    gate = jnp.dot(every, w_gate[0], preferred_element_type=jnp.float32)
    up = jnp.dot(every, w_up[0], preferred_element_type=jnp.float32)
    hidden = (jax.nn.silu(gate) * up * mine).astype(jnp.bfloat16)
    part = jnp.dot(hidden, w_down[0], preferred_element_type=jnp.float32).astype(jnp.bfloat16)
    moe = lax.psum_scatter(part, ("expert", "tensor"), scatter_dimension=0, tiled=True)
    mixed = (stream.astype(jnp.float32) + moe.astype(jnp.float32)).astype(jnp.bfloat16)
    return (
        lax.all_gather(mixed, "tensor", axis=0, tiled=True),
        lax.all_gather(logits, "tensor", axis=0, tiled=True),
    )

def shards_paired(
    attn_out,
    residual,
    o_weight,
    norm_gain,
    router_weight,
    expert_idx,
    combine,
    w_gate,
    w_up,
    w_down,
):
    y = lax.axis_index("tensor")
    me = lax.axis_index("expert")
    outer = lax.axis_size("expert") // 4
    rows = residual.shape[0] // 2
    width = residual.shape[1]
    expert_count = router_weight.shape[1]
    bf16 = jnp.bfloat16

    def take(array, at):
        return lax.dynamic_slice_in_dim(array, at * rows, rows, 0)

    experts = jnp.arange(expert_count, dtype=jnp.int32)
    dense = jnp.sum(
        jnp.where(take(expert_idx, y)[:, :, None] == experts, take(combine, y)[:, :, None], 0.0),
        axis=1,
    )
    high = dense.astype(bf16)
    low = (dense - high.astype(jnp.float32)).astype(bf16)
    extra = jnp.pad(jnp.concatenate([high, low], axis=1), ((0, 0), (0, -2 * expert_count % 128)))

    pieces = []
    cut = width // 4
    for i in range(4):
        partial = jnp.dot(
            attn_out, o_weight[:, i * cut:(i + 1) * cut], preferred_element_type=jnp.float32
        ).astype(bf16)
        came = lax.ppermute(take(partial, 1 - y), "tensor", [(0, 1), (1, 0)])
        pieces.append(take(partial, y).astype(jnp.float32) + came.astype(jnp.float32))
    projected = jnp.concatenate(pieces, axis=1)
    stream = (take(residual, y).astype(jnp.float32) + projected).astype(bf16)
    normed = rms_scaled(stream, norm_gain)
    hidden, logits = gather_hidden(normed, extra, w_gate[0], w_up[0], router_weight, outer)
    mixed = experts_home(hidden, w_down[0], stream, outer)
    return mixed.reshape(2 * rows, width), logits


def solution(mesh):
    in_specs = (
        P("expert", "tensor"),
        P("expert", None),
        P("tensor", None),
        P(),
        P(),
        P("expert", None),
        P("expert", None),
        P("expert", None, "tensor"),
        P("expert", None, "tensor"),
        P("expert", "tensor", None),
    )
    out_specs = (P("expert", None), P("expert", None))
    paired = mesh.shape["tensor"] == 2 and mesh.shape["expert"] % 4 == 0
    paired = paired and mesh.shape["expert"] > 4
    body = shards_paired if paired else shards
    return jax.shard_map(body, mesh=mesh, in_specs=in_specs, out_specs=out_specs, check_vma=False)
```
